768 devices in a mesh: section: 12 (over z), dp: 4 (over y_hi), tensor: 16 (over y_lo, x, core).
Axes of the slice: x: 4, y: 8 (y_hi: 4, y_lo: 2; y = y_hi * 2 + y_lo), z: 12, core: 2. Of those that a mesh axis runs over, the one named last changes fastest.
Arguments:
- context: bfloat16 [12, 2048, 8192], P('section', 'dp', 'tensor'), may hold values from -6 to 6
- residual: bfloat16 [12, 2048, 8192], P('section', 'tensor', 'dp')
- out_weight: bfloat16 [12, 8192, 8192], P('section', 'tensor', 'dp'), may hold values from -0.0625 to 0.0625
- norm_gain: float32 [12, 8192], P('section'), may hold values from 0.25 to 1.75
- valid_tokens: int32 [12], P('section'), may hold values from 1024 to 2048, as said below
Outputs:
- normed: bfloat16 [12, 2048, 8192], P('section', 'tensor', 'dp')
- handoff: bfloat16 [12, 2048, 8192], P('section', 'tensor', 'dp')
The draws below stay inside these ranges and needn't reach their ends.
Inputs may be any that keep to these rules, and one draw needn't show every extreme that they name: `valid_tokens`: some section's micro-batch is full in every draw.
All inputs are finite; a program needn't handle non-finite values.
Results may differ from the reference program's by a relative error of at most 0.018.
Values may be sent and summed in bfloat16 or wider, within the bound.
No kernel may reach another device: no remote copies, remote signals or barrier semaphores. Data moves between devices by JAX's collectives and lax.ppermute only.
A program may use at most 64 MiB of HBM per device.

```python
import jax
import jax.numpy as jnp
from jax import lax

D = 8192
TOKS = 2048
N_SECTION = 12
N_TENSOR = 16


def draw_residual(key, part):
    key = jax.random.fold_in(key, 11)
    key_val, key_row = jax.random.split(key, 2)
    values = jax.random.normal(key_val, (N_SECTION, TOKS, D), jnp.float32)
    row_exp = jax.random.uniform(key_row, (N_SECTION, TOKS, 1), jnp.float32, -0.5, 0.5)
    col_exp = jnp.arange(D, dtype=jnp.float32)[None, None, :] / D - 0.5
    return (values * 10.0 ** row_exp * 10.0 ** col_exp).astype(jnp.bfloat16)


def draw_valid_tokens(key, part):
    key = jax.random.fold_in(key, 23)
    key_len, key_full = jax.random.split(key)
    lengths = jax.random.randint(key_len, (N_SECTION,), TOKS // 2, TOKS + 1)
    full = jax.random.randint(key_full, (), 0, N_SECTION)
    return lengths.at[full].set(TOKS).astype(jnp.int32)


def block_scale(key, extent, pieces, smallest, largest):
    level = 1.0
    for dim, shards_of in pieces:
        steps = jax.random.uniform(jax.random.fold_in(jax.random.fold_in(key, 6), dim), (shards_of,), jnp.float32, smallest / len(pieces), largest / len(pieces))
        level = level * jnp.repeat(jnp.exp(steps), extent[dim] // shards_of).reshape((-1,) + (1,) * (len(extent) - 1 - dim))
    return level


def bell_draw(key, shape, spread, most, cuts=(), held_as=jnp.bfloat16):
    entries = spread * jax.random.normal(key, shape, jnp.float32)
    if cuts:
        entries = entries * block_scale(key, shape, cuts, -0.22, 0.18)
    return jnp.clip(entries, -most, most).astype(held_as)


def setup_inputs(seed: int = 0) -> dict:
    seeds = jax.random.split(jax.random.key(seed), 6)
    return {
        "context": bell_draw(seeds[0], (N_SECTION, TOKS, D), 1.0, 6.0, ((0, 12), (1, 4), (2, 16))),
        "residual": draw_residual(jax.random.fold_in(seeds[5], 71), 0),
        "out_weight": bell_draw(seeds[2], (N_SECTION, D, D), D ** -0.5, 0.0625, ((0, 12), (1, 16), (2, 4))),
        "norm_gain": jnp.clip(1.0 + 0.15 * jax.random.normal(seeds[3], (N_SECTION, D), jnp.float32), 0.25, 1.75),
        "valid_tokens": draw_valid_tokens(jax.random.fold_in(seeds[5], 71), 0),
    }


def one_section(inputs):
    context_s, residual_s, weight_s, gain_s, valid_s = inputs
    width = D // N_TENSOR
    groups = context_s.reshape(TOKS, N_TENSOR, width).transpose(1, 0, 2)
    weights = weight_s.reshape(N_TENSOR, width, D)

    def add_group(total, pair):
        part = jnp.dot(pair[0], pair[1], preferred_element_type=jnp.float32).astype(jnp.bfloat16)
        part = lax.optimization_barrier(part)
        return (total + part.astype(jnp.float32), None)
    attn, _ = lax.scan(add_group, jnp.zeros((TOKS, D), jnp.float32), (groups, weights))
    hidden = residual_s.astype(jnp.float32) + attn
    mean_sq = lax.optimization_barrier(jnp.mean(hidden * hidden, axis=1, keepdims=True))
    keep = (jnp.arange(TOKS, dtype=jnp.int32) < valid_s)[:, None]
    normed = jnp.where(keep, hidden * lax.rsqrt(mean_sq + 1e-06) * gain_s[None, :], 0.0).astype(jnp.bfloat16)
    outgoing = jnp.where(keep, hidden, 0.0).astype(jnp.bfloat16)
    return (normed, outgoing)

def reference(context, residual, out_weight, norm_gain, valid_tokens):
    normed, outgoing = lax.map(one_section, (context, residual, out_weight, norm_gain, valid_tokens))
    handoff = jnp.concatenate([jnp.zeros_like(outgoing[:1]), outgoing[:-1]], axis=0)
    return (normed, handoff)
```

```python
import functools

import jax
import jax.numpy as jnp
from jax import lax
from jax.experimental import pallas as pl
from jax.experimental.pallas import tpu as pltpu
from jax.sharding import Mesh, PartitionSpec as P

CHUNKS = 2
HALF = 1024
WIDE = 256


def project(pos, own, right, left, far_r, far_l, w_own, w_oth, w_own_b, w_oth_b, keep_a, send_a, keep_b, send_b, rows_a, rows_b):
    step = pl.program_id(0)

    @pl.when(step == 0)
    def _():
        d, x = pos[0], pos[1]
        outer = jnp.logical_or(x == 0, x == 3).astype(jnp.int32)
        for source, shift, xls in ((own, 0, (0, 1)), (right, 3, (0, 1)), (left, 1, (0, 1)), (far_r, 2, (0,)), (far_l, 2, (1,))):
            dd = lax.rem(d + shift, 4)
            odd, ylo = dd % 2, dd // 2
            for xl in xls:
                block = source[xl] if len(xls) == 2 else source[...]
                same = (odd == xl).astype(jnp.int32)
                slot_a = jnp.where(same == outer, 0, 4) + odd * 2 + ylo
                slot_b = jnp.where(odd == x // 2, 0, 4) + xl * 2 + ylo
                rows_a[slot_a] = block
                rows_b[slot_b] = block

    for rows, first, second, keep, send in ((rows_a, w_own, w_oth, keep_a, send_a), (rows_b, w_own_b, w_oth_b, keep_b, send_b)):
        lhs = rows[...].reshape(-1, 2 * w_own.shape[0])
        k = w_own.shape[0]
        value = jnp.dot(lhs[:, :k], first[...], preferred_element_type=jnp.float32)
        value += jnp.dot(lhs[:, k:], second[...], preferred_element_type=jnp.float32)
        value = value.astype(jnp.bfloat16)
        half = value.shape[0] // 2
        keep[...] = value[:half]
        send[...] = value[half:]


def projected(pos, own, right, left, far_r, far_l, w_own, w_oth):
    r, k2 = own.shape[1], own.shape[2]
    k = k2 // 2
    whole = lambda a: pl.BlockSpec(a.shape, lambda j, p: (0,) * a.ndim)
    tile = lambda off: pl.BlockSpec((k, WIDE), lambda j, p: (0, j + off))
    steps = HALF // WIDE
    out = jax.ShapeDtypeStruct((4 * r, HALF), jnp.bfloat16)
    return pl.pallas_call(
        project,
        grid_spec=pltpu.PrefetchScalarGridSpec(
            num_scalar_prefetch=1,
            grid=(steps,),
            in_specs=[whole(own), whole(right), whole(left), whole(far_r), whole(far_l), tile(0), tile(0), tile(steps), tile(steps)],
            out_specs=[pl.BlockSpec((4 * r, WIDE), lambda j, p: (0, j))] * 4,
            scratch_shapes=[pltpu.VMEM((8, r, k2), jnp.bfloat16)] * 2,
        ),
        out_shape=[out] * 4,
        cost_estimate=pl.CostEstimate(flops=2 * 8 * r * k2 * 2 * HALF, bytes_accessed=2 * (8 * r * k2 + 2 * k2 * HALF + 16 * r * HALF), transcendentals=0),
        compiler_params=pltpu.CompilerParams(vmem_limit_bytes=40 * 2**20),
    )(pos, own, right, left, far_r, far_l, w_own, w_oth, w_own, w_oth)


def split_sum(pos, keep_a, got_a, keep_b, got_b, mine_a, give_a, mine_b, give_b):
    x = pos[1]
    for keep, got, mine, give, rank in ((keep_a, got_a, mine_a, give_a, x // 2), (keep_b, got_b, mine_b, give_b, x % 2)):
        mine[...] = (keep[rank].astype(jnp.float32) + got[rank].astype(jnp.float32)).astype(jnp.bfloat16)
        give[...] = (keep[1 - rank].astype(jnp.float32) + got[1 - rank].astype(jnp.float32)).astype(jnp.bfloat16)


def split_summed(pos, keep_a, got_a, keep_b, got_b):
    n, m = keep_a.shape
    args = [a.reshape(2, n // 2, m) for a in (keep_a, got_a, keep_b, got_b)]
    vmem = pl.BlockSpec(memory_space=pltpu.VMEM)
    return pl.pallas_call(
        split_sum,
        in_specs=[pl.BlockSpec(memory_space=pltpu.SMEM)] + [vmem] * 4,
        out_specs=[vmem] * 4,
        out_shape=[jax.ShapeDtypeStruct((n // 2, m), jnp.bfloat16)] * 4,
        cost_estimate=pl.CostEstimate(flops=2 * n * m, bytes_accessed=2 * n * m * 6, transcendentals=0),
    )(pos, *args)


def on_device(sections, context, residual, out_weight, norm_gain, valid_tokens):
    d, ylo, x, core = (lax.axis_index(a) for a in ("dp", "ylo", "x", "core"))
    pos = jnp.stack([d, x]).astype(jnp.int32)
    width = context.shape[2]
    rows = residual.shape[1]
    r = rows // CHUNKS
    ring = lambda k: [(i, (i + k) % 4) for i in range(4)]
    near, mirror, swap = [(i, i ^ 1) for i in range(4)], [(i, 3 - i) for i in range(4)], [(0, 1), (1, 0)]

    tokens = context.reshape(2, 2, rows, width)
    mine = lax.dynamic_index_in_dim(tokens, core, 1, keepdims=False)
    theirs = lax.dynamic_index_in_dim(tokens, 1 - core, 1, keepdims=False)
    both = jnp.concatenate([mine, lax.ppermute(theirs, "core", swap)], axis=-1)
    w_own = out_weight[0]
    w_oth = lax.ppermute(w_own, "core", swap)

    outs, squares, moved = [], [], []
    hs = []
    for c in range(CHUNKS):
        own = both[:, c * r:(c + 1) * r]
        right = lax.ppermute(own, "dp", ring(1))
        left = lax.ppermute(own, "dp", ring(3))
        far_r = lax.ppermute(right[0], "dp", ring(1))
        far_l = lax.ppermute(left[1], "dp", ring(3))
        keep_a, send_a, keep_b, send_b = projected(pos, own, right, left, far_r, far_l, w_own, w_oth)
        got_a = lax.ppermute(send_a, "x", near)
        got_b = lax.ppermute(send_b, "x", mirror)
        keep_a, send_a, keep_b, send_b = split_summed(pos, keep_a, got_a, keep_b, got_b)
        got_a = lax.ppermute(send_a, "x", mirror)
        got_b = lax.ppermute(send_b, "x", near)
        total = jnp.concatenate([
            (keep_a.astype(jnp.float32) + got_a.astype(jnp.float32)).reshape(2, r, HALF),
            (keep_b.astype(jnp.float32) + got_b.astype(jnp.float32)).reshape(2, r, HALF)], axis=-1)
        stay = lax.dynamic_index_in_dim(total, ylo, 0, keepdims=False)
        go = lax.dynamic_index_in_dim(total, 1 - ylo, 0, keepdims=False).astype(jnp.bfloat16)
        attn = stay + lax.ppermute(go, "ylo", swap).astype(jnp.float32)
        h = residual[0, c * r:(c + 1) * r].astype(jnp.float32) + attn
        row = ((ylo * 4 + x) * 2 + core) * rows + c * r + jnp.arange(r, dtype=jnp.int32)
        live = (row < valid_tokens[0])[:, None]
        out = jnp.where(live, h, 0.0).astype(jnp.bfloat16)
        moved.append(lax.ppermute(out, "section", [(s, s + 1) for s in range(sections - 1)]))
        hs.append(jnp.where(live, h, 0.0))
        squares.append(jnp.sum(h * h, axis=1))
    square = jnp.concatenate(squares)[None]
    square = square + lax.ppermute(square, "dp", near)
    square = square + lax.ppermute(square, "dp", [(i, i ^ 2) for i in range(4)])
    scale = lax.rsqrt(square[0] / 8192.0 + 1e-06)
    gain = lax.dynamic_slice_in_dim(norm_gain[0], d * residual.shape[2], residual.shape[2])
    normed = (jnp.concatenate(hs) * scale[:, None] * gain[None, :]).astype(jnp.bfloat16)
    return normed[None], jnp.concatenate(moved)[None]


def solution(mesh):
    sections = mesh.devices.shape[0]
    fine = Mesh(mesh.devices.reshape(sections, 4, 2, 4, 2), ("section", "dp", "ylo", "x", "core"))
    tensor = ("ylo", "x", "core")
    placed = (P("section", "dp", tensor), P("section", tensor, "dp"), P("section", tensor, "dp"), P("section", None), P("section"))
    return jax.shard_map(
        functools.partial(on_device, sections),
        mesh=fine,
        in_specs=placed,
        out_specs=(P("section", tensor, "dp"), P("section", tensor, "dp")),
        check_vma=False,
    )
```

```python
import functools

import jax
import jax.numpy as jnp
from jax import lax
from jax.experimental import pallas as pl
from jax.experimental.pallas import tpu as pltpu
from jax.sharding import Mesh, PartitionSpec as P

WIDE = 512
PARTS = 4


def project(*refs, places, first_rel, added):
    n = len(places)
    sources, weights = refs[:n], refs[n:n + 2]
    before = refs[n + 2] if added else None
    out, rows, held, base, result, in_sem, out_sem = refs[-7:]
    d, me = lax.axis_index("dp"), lax.axis_index("tensor") % 4
    k, columns = weights[0].shape
    copies = []

    def fetch(source, target):
        copies.append(pltpu.make_async_copy(source, target, in_sem.at[len(copies)]))
        copies[-1].start()

    for source, (shift, begin) in zip(sources, places):
        slot = lax.rem(d + shift, PARTS)
        for i in range(2):
            fetch(source.at[me ^ (first_rel + i)], rows.at[slot, pl.ds(begin, source.shape[1]), pl.ds(i * k, k)])
    first = len(copies)
    each = 3 if added else 2
    for at in range(0, columns, WIDE):
        for i, weight in enumerate(weights):
            fetch(weight.at[:, pl.ds(at, WIDE)], held.at[pl.ds(i * k, k), pl.ds(at, WIDE)])
        if added:
            fetch(before.at[:, :, pl.ds(at, WIDE)], base.at[:, :, pl.ds(at, WIDE)])
    for copy in copies[:first]:
        copy.wait()
    lhs = rows[...].reshape(-1, 2 * k)
    sent = []
    for j, at in enumerate(range(0, columns, WIDE)):
        for copy in copies[first + each * j:first + each * (j + 1)]:
            copy.wait()
        value = jnp.dot(lhs, held[:, at:at + WIDE], preferred_element_type=jnp.float32).reshape(PARTS, -1, WIDE)
        if added:
            value += base[:, :, at:at + WIDE]
        result[:, :, at:at + WIDE] = value.astype(result.dtype)
        sent.append(pltpu.make_async_copy(result.at[:, :, pl.ds(at, WIDE)], out.at[:, :, pl.ds(at, WIDE)], out_sem.at[j]))
        sent[-1].start()
    for copy in sent:
        copy.wait()


def projected(places, first_rel, sources, weights, before, rows):
    k, columns = weights[0].shape
    tiles = columns // WIDE
    added = before is not None
    kind = jnp.bfloat16 if added else jnp.float32
    anywhere = pl.BlockSpec(memory_space=pl.ANY)
    operands = [*sources, *weights] + ([before] if added else [])
    return pl.pallas_call(
        functools.partial(project, places=places, first_rel=first_rel, added=added),
        in_specs=[anywhere] * len(operands),
        out_specs=anywhere,
        out_shape=jax.ShapeDtypeStruct((PARTS, rows, columns), kind),
        scratch_shapes=[
            pltpu.VMEM((PARTS, rows, 2 * k), jnp.bfloat16),
            pltpu.VMEM((2 * k, columns), jnp.bfloat16),
            pltpu.VMEM((PARTS, rows, columns) if added else (1, 8, 128), jnp.float32),
            pltpu.VMEM((PARTS, rows, columns), kind),
            pltpu.SemaphoreType.DMA((2 * len(sources) + 3 * tiles,)),
            pltpu.SemaphoreType.DMA((tiles,)),
        ],
        cost_estimate=pl.CostEstimate(
            flops=2 * PARTS * rows * 2 * k * columns,
            bytes_accessed=2 * (PARTS * rows * 2 * k + 2 * k * columns + 3 * PARTS * rows * columns),
            transcendentals=0),
        compiler_params=pltpu.CompilerParams(vmem_limit_bytes=24 * 2**20),
    )(*operands)


def after(value, *others):
    return lax.optimization_barrier((value, *others))[0]


def on_device(sections, context, residual, out_weight, norm_gain, valid_tokens):
    d = lax.axis_index("dp")
    t = lax.axis_index("tensor")
    width = context.shape[2]
    rows = residual.shape[1]
    r = rows // 2
    swap = [(i, i ^ 1) for i in range(16)]
    pair = [(i, i ^ 2) for i in range(16)]
    up = [(i, (i + 1) % 4) for i in range(4)]
    down = [(i, (i - 1) % 4) for i in range(4)]
    quads = [[4 * g + i for i in range(4)] for g in range(4)]
    across = [[4 * g + i for g in range(4)] for i in range(4)]

    tokens = lax.all_to_all(context.reshape(4, rows, width), "tensor", 0, 0, axis_index_groups=quads, tiled=True)
    weight = out_weight[0]
    near = [lax.ppermute(after(weight, tokens), "tensor", pair)]

    own_a, own_b = tokens[:, :r], tokens[:, r:]
    right_a = lax.ppermute(own_a, "dp", up)
    left_b = lax.ppermute(own_b, "dp", down)
    left_a = lax.ppermute(own_a, "dp", down)
    right_b = lax.ppermute(own_b, "dp", up)
    far_a = lax.ppermute(right_a, "dp", up)
    far_b = lax.ppermute(left_b, "dp", down)
    sources = [tokens, right_a, right_b, left_a, left_b, far_a, far_b]
    places = [(0, 0), (3, 0), (3, r), (1, 0), (1, r), (2, 0), (2, r)]
    w_core = lax.ppermute(weight, "tensor", swap)
    cross = [lax.ppermute(after(w, *sources), "tensor", swap) for w in near]

    part = projected(tuple(places), 0, sources, [weight, w_core], None, rows)
    part = projected(tuple(places), 2, sources, [*near, *cross], part, rows)
    got = lax.all_to_all(part, "tensor", 0, 0, axis_index_groups=across, tiled=True)
    h = residual[0].astype(jnp.float32) + jnp.sum(got.astype(jnp.float32), axis=0)
    row = t * rows + jnp.arange(rows, dtype=jnp.int32)
    live = (row < valid_tokens[0])[:, None]
    kept = jnp.where(live, h, 0.0)
    moved = lax.ppermute(kept.astype(jnp.bfloat16), "section", [(s, s + 1) for s in range(sections - 1)])
    square = jnp.sum(h * h, axis=1)[None]
    square = jnp.broadcast_to(square[None], (4, 1, rows))
    square = jnp.sum(lax.all_to_all(square, "dp", 0, 0, tiled=True), axis=0)
    scale = lax.rsqrt(square[0] / 8192.0 + 1e-06)
    gain = lax.dynamic_slice_in_dim(norm_gain[0], d * residual.shape[2], residual.shape[2])
    kept = after(kept, moved)
    normed = (kept * scale[:, None] * gain[None, :]).astype(jnp.bfloat16)
    return normed[None], moved[None]


def solution(mesh):
    placed = (
        P("section", "dp", "tensor"),
        P("section", "tensor", "dp"),
        P("section", "tensor", "dp"),
        P("section", None),
        P("section"),
    )
    return jax.shard_map(
        functools.partial(on_device, mesh.devices.shape[0]),
        mesh=mesh,
        in_specs=placed,
        out_specs=(P("section", "tensor", "dp"), P("section", "tensor", "dp")),
        check_vma=False,
    )
```

```python
import functools

import jax
import jax.numpy as jnp
from jax import lax
from jax.experimental import pallas as pl
from jax.experimental.pallas import tpu as pltpu
from jax.sharding import Mesh, PartitionSpec as P

WIDE = 512
CUT = 1024
PARTS = 4


def project(*refs, places, first_rel, going):
    n = len(places)
    sources, weights = refs[:n], refs[n:n + 2]
    added = going is not None
    before = refs[n + 2] if added else None
    outs, (rows, held, base, result, in_sem, out_sem) = refs[n + 2 + added:-6], refs[-6:]
    d, t = lax.axis_index("dp"), lax.axis_index("tensor")
    ylo, xh, me = t // 8, (t // 4) % 2, t % 4
    k, columns = weights[0].shape
    copies = []

    def fetch(source, target):
        copies.append(pltpu.make_async_copy(source, target, in_sem.at[len(copies)]))
        copies[-1].start()

    for source, (shift, begin) in zip(sources, places):
        slot = lax.rem(d + shift, PARTS)
        order = me ^ (((slot % 2) ^ xh) * 2)
        for i in range(2):
            fetch(source.at[order ^ (first_rel + i)], rows.at[slot, pl.ds(begin, source.shape[1]), pl.ds(i * k, k)])
    first = len(copies)
    if going:
        wanted = ([(1 - ylo) * 2 + i for i in range(2)], [i * 2 + 1 - xh for i in range(2)])
    else:
        wanted = ([ylo * 2 + i for i in range(2)], [i * 2 + xh for i in range(2)])
    each = 4 if added else 2
    for at in range(0, columns, WIDE):
        for i, weight in enumerate(weights):
            fetch(weight.at[:, pl.ds(at, WIDE)], held.at[pl.ds(i * k, k), pl.ds(at, WIDE)])
        if added:
            for i, block in enumerate(wanted[at // CUT]):
                fetch(before.at[block, :, pl.ds(at, WIDE)], base.at[i, :, pl.ds(at, WIDE)])
    for copy in copies[:first]:
        copy.wait()
    sent = []
    for j, at in enumerate(range(0, columns, WIDE)):
        if not added:
            lhs = rows[...].reshape(-1, 2 * k)
        elif at % CUT == 0:
            lhs = jnp.concatenate([rows[block] for block in wanted[at // CUT]], axis=0)
        for copy in copies[first + each * j:first + each * (j + 1)]:
            copy.wait()
        value = jnp.dot(lhs, held[:, at:at + WIDE], preferred_element_type=jnp.float32).reshape(result.shape[0], -1, WIDE)
        if added:
            value += base[:, :, at:at + WIDE].astype(jnp.float32)
        result[:, :, at:at + WIDE] = value.astype(result.dtype)
        target, to = (outs[at // CUT], at % CUT) if added else (outs[0], at)
        sent.append(pltpu.make_async_copy(result.at[:, :, pl.ds(at, WIDE)], target.at[:, :, pl.ds(to, WIDE)], out_sem.at[j]))
        sent[-1].start()
    for copy in sent:
        copy.wait()


def projected(places, first_rel, sources, weights, before, rows, going=None):
    k, columns = weights[0].shape
    tiles = columns // WIDE
    added = going is not None
    parts = 2 if added else PARTS
    shapes = [(2, rows, CUT)] * 2 if added else [(PARTS, rows, columns)]
    anywhere = pl.BlockSpec(memory_space=pl.ANY)
    operands = [*sources, *weights] + ([before] if added else [])
    return pl.pallas_call(
        functools.partial(project, places=places, first_rel=first_rel, going=going),
        in_specs=[anywhere] * len(operands),
        out_specs=[anywhere] * len(shapes),
        out_shape=[jax.ShapeDtypeStruct(shape, jnp.bfloat16 if added else jnp.bfloat16) for shape in shapes],
        scratch_shapes=[
            pltpu.VMEM((PARTS, rows, 2 * k), jnp.bfloat16),
            pltpu.VMEM((2 * k, columns), jnp.bfloat16),
            pltpu.VMEM((2, rows, columns) if added else (1, 16, 128), jnp.bfloat16),
            pltpu.VMEM((parts, rows, columns), jnp.bfloat16 if added else jnp.bfloat16),
            pltpu.SemaphoreType.DMA((2 * len(sources) + 4 * tiles,)),
            pltpu.SemaphoreType.DMA((tiles,)),
        ],
        cost_estimate=pl.CostEstimate(
            flops=2 * parts * rows * 2 * k * columns,
            bytes_accessed=2 * (PARTS * rows * 2 * k + 2 * k * columns + 2 * parts * rows * columns),
            transcendentals=0),
        compiler_params=pltpu.CompilerParams(vmem_limit_bytes=24 * 2**20),
    )(*operands)


def split_sum(keep, got, mine, give, *, over):
    t = lax.axis_index("tensor")
    here = (t // 4) % 2 if over == "x" else t // 8
    mine[...] = keep[here].astype(jnp.float32) + got[here].astype(jnp.float32)
    give[...] = (keep[1 - here].astype(jnp.float32) + got[1 - here].astype(jnp.float32)).astype(jnp.bfloat16)


def split_summed(keep, got, over):
    _, n, m = keep.shape
    vmem = pl.BlockSpec(memory_space=pltpu.VMEM)
    return pl.pallas_call(
        functools.partial(split_sum, over=over),
        in_specs=[vmem] * 2,
        out_specs=[vmem] * 2,
        out_shape=[jax.ShapeDtypeStruct((n, m), kind) for kind in (jnp.float32, jnp.bfloat16)],
        cost_estimate=pl.CostEstimate(flops=2 * n * m, bytes_accessed=11 * n * m, transcendentals=0),
        compiler_params=pltpu.CompilerParams(vmem_limit_bytes=8 * 2**20),
    )(keep, got)


def after(value, *others):
    return lax.optimization_barrier((value, *others))[0]


def on_device(sections, context, residual, out_weight, norm_gain, valid_tokens):
    d = lax.axis_index("dp")
    t = lax.axis_index("tensor")
    width = context.shape[2]
    rows = residual.shape[1]
    r = rows // 2
    swap = [(i, i ^ 1) for i in range(16)]
    pair = [(i, i ^ 2) for i in range(16)]
    up = [(i, (i + 1) % 4) for i in range(4)]
    down = [(i, (i - 1) % 4) for i in range(4)]
    quads = [[16 * dd + 4 * g + (i ^ (2 * ((dd ^ g) % 2))) for i in range(4)] for dd in range(4) for g in range(4)]
    across = [[4 * g + i for g in range(4)] for i in range(4)]

    tokens = lax.all_to_all(context.reshape(4, rows, width), ("dp", "tensor"), 0, 0, axis_index_groups=quads, tiled=True)
    weight = out_weight[0]
    near = [lax.ppermute(after(weight, tokens), "tensor", pair)]

    own_a, own_b = tokens[:, :r], tokens[:, r:]
    right_a = lax.ppermute(own_a, "dp", up)
    left_b = lax.ppermute(own_b, "dp", down)
    left_a = lax.ppermute(own_a, "dp", down)
    right_b = lax.ppermute(own_b, "dp", up)
    far_a = lax.ppermute(right_a, "dp", up)
    far_b = lax.ppermute(left_b, "dp", down)
    sources = [tokens, right_a, right_b, left_a, left_b, far_a, far_b]
    places = [(0, 0), (3, 0), (3, r), (1, 0), (1, r), (2, 0), (2, r)]
    w_core = lax.ppermute(weight, "tensor", swap)
    cross = [lax.ppermute(after(w, *sources), "tensor", swap) for w in near]

    (part,) = projected(tuple(places), 0, sources, [weight, w_core], None, rows)
    send_a, send_b = projected(tuple(places), 2, sources, [*near, *cross], part, rows, True)
    keep_a, keep_b = projected(tuple(places), 2, sources, [*near, *cross], part, rows, False)
    over_y = [(i, i ^ 8) for i in range(16)]
    over_x = [(i, i ^ 6) for i in range(16)]
    got_b = lax.ppermute(send_b, "tensor", over_x)
    got_a = lax.ppermute(send_a, "tensor", over_y)
    keep_b, send_b = split_summed(keep_b, got_b, "y")
    keep_a, send_a = split_summed(keep_a, got_a, "x")
    got_a = lax.ppermute(send_a, "tensor", over_x)
    got_b = lax.ppermute(send_b, "tensor", over_y)
    attn = jnp.concatenate([keep_a + got_a.astype(jnp.float32), keep_b + got_b.astype(jnp.float32)], axis=1)
    h = residual[0].astype(jnp.float32) + attn
    row = t * rows + jnp.arange(rows, dtype=jnp.int32)
    live = (row < valid_tokens[0])[:, None]
    kept = jnp.where(live, h, 0.0)
    onward = [(s, s + 1) for s in range(sections - 1)]
    sending = kept.astype(jnp.bfloat16)
    square = jnp.sum(h * h, axis=1)[None]
    GATE = 0
    if GATE:
        begun = lax.ppermute(sending[:GATE], "section", onward)
        moved = jnp.concatenate([begun, lax.ppermute(sending[GATE:], "section", onward)])
        square = after(square, begun)
    else:
        moved = lax.ppermute(sending, "section", onward)
    square = lax.psum(square, "dp")
    scale = lax.rsqrt(square[0] / 8192.0 + 1e-06)
    gain = lax.dynamic_slice_in_dim(norm_gain[0], d * residual.shape[2], residual.shape[2])
    kept = after(kept, moved)
    normed = (kept * scale[:, None] * gain[None, :]).astype(jnp.bfloat16)
    return normed[None], moved[None]


def solution(mesh):
    placed = (
        P("section", "dp", "tensor"),
        P("section", "tensor", "dp"),
        P("section", "tensor", "dp"),
        P("section", None),
        P("section"),
    )
    return jax.shard_map(
        functools.partial(on_device, mesh.devices.shape[0]),
        mesh=mesh,
        in_specs=placed,
        out_specs=(P("section", "tensor", "dp"), P("section", "tensor", "dp")),
        check_vma=False,
    )
```

```python
import functools

import jax
import jax.numpy as jnp
from jax import lax
from jax.experimental import pallas as pl
from jax.experimental.pallas import tpu as pltpu
from jax.sharding import Mesh, PartitionSpec as P

WIDE = 512
CUT = 1024
TILES = (512, 512, 512, 512)
PARTS = 4


def tiles_of(columns, added):
    widths = TILES if added else (WIDE,) * (columns // WIDE)
    return [(sum(widths[:i]), width) for i, width in enumerate(widths)]


def project(*refs, places, first_rel, going):
    n = len(places)
    sources, weights = refs[:n], refs[n:n + 2]
    added = going is not None
    before = refs[n + 2] if added else None
    outs, (rows, held, base, result, in_sem, out_sem) = refs[n + 2 + added:-6], refs[-6:]
    d, t = lax.axis_index("dp"), lax.axis_index("tensor")
    ylo, xh, me = t // 8, (t // 4) % 2, t % 4
    k, columns = weights[0].shape
    copies = []

    def fetch(source, target):
        copies.append(pltpu.make_async_copy(source, target, in_sem.at[len(copies)]))
        copies[-1].start()

    for source, (shift, begin) in zip(sources, places):
        slot = lax.rem(d + shift, PARTS)
        for i in range(2):
            fetch(source.at[first_rel + i], rows.at[slot, pl.ds(begin, source.shape[1]), pl.ds(i * k, k)])
    first = len(copies)
    if going:
        wanted = ([(1 - ylo) * 2 + i for i in range(2)], [i * 2 + 1 - xh for i in range(2)])
    else:
        wanted = ([ylo * 2 + i for i in range(2)], [i * 2 + xh for i in range(2)])
    each = 4 if added else 2
    tiles = tiles_of(columns, added)
    for at, width in tiles:
        for i, weight in enumerate(weights):
            fetch(weight.at[:, pl.ds(at, width)], held.at[pl.ds(i * k, k), pl.ds(at, width)])
        if added:
            for i, block in enumerate(wanted[at >= CUT]):
                fetch(before.at[block, :, pl.ds(at, width)], base.at[i, :, pl.ds(at, width)])
    for copy in copies[:first]:
        copy.wait()
    sent = []
    for j, (at, width) in enumerate(tiles):
        here = pl.ds(at, width)
        if not added:
            lhs = rows[...].reshape(-1, 2 * k)
        elif at in (0, CUT):
            lhs = jnp.concatenate([rows[block] for block in wanted[at >= CUT]], axis=0)
        for copy in copies[first + each * j:first + each * (j + 1)]:
            copy.wait()
        value = jnp.dot(lhs, held[:, here], preferred_element_type=jnp.float32).reshape(result.shape[0], -1, width)
        if added:
            value += base[:, :, here].astype(jnp.float32)
        result[:, :, here] = value.astype(result.dtype)
        target, to = (outs[1], at - CUT) if added and at >= CUT else (outs[0], at)
        sent.append(pltpu.make_async_copy(result.at[:, :, here], target.at[:, :, pl.ds(to, width)], out_sem.at[j]))
        sent[-1].start()
    for copy in sent:
        copy.wait()


def projected(places, first_rel, sources, weights, before, rows, going=None):
    k, columns = weights[0].shape
    added = going is not None
    tiles = len(tiles_of(columns, added))
    parts = 2 if added else PARTS
    shapes = [(2, rows, CUT), (2, rows, columns - CUT)] if added else [(PARTS, rows, columns)]
    anywhere = pl.BlockSpec(memory_space=pl.ANY)
    operands = [*sources, *weights] + ([before] if added else [])
    return pl.pallas_call(
        functools.partial(project, places=places, first_rel=first_rel, going=going),
        in_specs=[anywhere] * len(operands),
        out_specs=[anywhere] * len(shapes),
        out_shape=[jax.ShapeDtypeStruct(shape, jnp.bfloat16 if added else jnp.bfloat16) for shape in shapes],
        scratch_shapes=[
            pltpu.VMEM((PARTS, rows, 2 * k), jnp.bfloat16),
            pltpu.VMEM((2 * k, columns), jnp.bfloat16),
            pltpu.VMEM((2, rows, columns) if added else (1, 16, 128), jnp.bfloat16),
            pltpu.VMEM((parts, rows, columns), jnp.bfloat16 if added else jnp.bfloat16),
            pltpu.SemaphoreType.DMA((2 * len(sources) + 4 * tiles,)),
            pltpu.SemaphoreType.DMA((tiles,)),
        ],
        cost_estimate=pl.CostEstimate(
            flops=2 * parts * rows * 2 * k * columns,
            bytes_accessed=2 * (PARTS * rows * 2 * k + 2 * k * columns + 2 * parts * rows * columns),
            transcendentals=0),
        compiler_params=pltpu.CompilerParams(vmem_limit_bytes=24 * 2**20),
    )(*operands)


def split_sum(keep, got, mine, give, *, over):
    t = lax.axis_index("tensor")
    here = (t // 4) % 2 if over == "x" else t // 8
    mine[...] = keep[here].astype(jnp.float32) + got[here].astype(jnp.float32)
    give[...] = (keep[1 - here].astype(jnp.float32) + got[1 - here].astype(jnp.float32)).astype(jnp.bfloat16)


def split_summed(keep, got, over):
    _, n, m = keep.shape
    vmem = pl.BlockSpec(memory_space=pltpu.VMEM)
    return pl.pallas_call(
        functools.partial(split_sum, over=over),
        in_specs=[vmem] * 2,
        out_specs=[vmem] * 2,
        out_shape=[jax.ShapeDtypeStruct((n, m), kind) for kind in (jnp.float32, jnp.bfloat16)],
        cost_estimate=pl.CostEstimate(flops=2 * n * m, bytes_accessed=11 * n * m, transcendentals=0),
        compiler_params=pltpu.CompilerParams(vmem_limit_bytes=8 * 2**20),
    )(keep, got)


def after(value, *others):
    return lax.optimization_barrier((value, *others))[0]


def on_device(sections, context, residual, out_weight, norm_gain, valid_tokens):
    d = lax.axis_index("dp")
    t = lax.axis_index("tensor")
    width = context.shape[2]
    rows = residual.shape[1]
    r = rows // 2
    swap = [(i, i ^ 1) for i in range(16)]
    pair = [(i, i ^ 2) for i in range(16)]
    up = [(i, (i + 1) % 4) for i in range(4)]
    down = [(i, (i - 1) % 4) for i in range(4)]
    quads = [[16 * dd + 4 * g + (i ^ (2 * ((dd ^ g) % 2))) for i in range(4)] for dd in range(4) for g in range(4)]
    across = [[4 * g + i for g in range(4)] for i in range(4)]

    pieces = context.reshape(4, rows, width)
    flip = 2 * ((d % 2) ^ ((t // 4) % 2))
    mine, along, across, corner = (lax.dynamic_index_in_dim(pieces, (t % 4) ^ rel ^ flip, 0, keepdims=False) for rel in range(4))
    got = lax.ppermute(jnp.stack([across, corner]), "tensor", pair)
    across, passed = got[0], got[1]
    along, corner = lax.ppermute(jnp.stack([along, passed]), "tensor", swap)
    tokens = jnp.stack([mine, along, across, corner])
    weight = out_weight[0]
    near = [lax.ppermute(after(weight, got), "tensor", pair)]

    own_a, own_b = tokens[:, :r], tokens[:, r:]
    right_a = lax.ppermute(own_a, "dp", up)
    left_b = lax.ppermute(own_b, "dp", down)
    left_a = lax.ppermute(own_a, "dp", down)
    right_b = lax.ppermute(own_b, "dp", up)
    far_a = lax.ppermute(right_a, "dp", up)
    far_b = lax.ppermute(left_b, "dp", down)
    sources = [tokens, right_a, right_b, left_a, left_b, far_a, far_b]
    places = [(0, 0), (3, 0), (3, r), (1, 0), (1, r), (2, 0), (2, r)]
    w_core = lax.ppermute(weight, "tensor", swap)
    cross = [lax.ppermute(after(w, *sources), "tensor", swap) for w in near]

    (part,) = projected(tuple(places), 0, sources, [weight, w_core], None, rows)
    send_a, send_b = projected(tuple(places), 2, sources, [*near, *cross], part, rows, True)
    keep_a, keep_b = projected(tuple(places), 2, sources, [*near, *cross], part, rows, False)
    over_y = [(i, i ^ 8) for i in range(16)]
    over_x = [(i, i ^ 6) for i in range(16)]
    got_b = lax.ppermute(send_b, "tensor", over_x)
    got_a = lax.ppermute(send_a, "tensor", over_y)
    keep_b, send_b = split_summed(keep_b, got_b, "y")
    keep_a, send_a = split_summed(keep_a, got_a, "x")
    got_a = lax.ppermute(send_a, "tensor", over_x)
    got_b = lax.ppermute(send_b, "tensor", over_y)
    attn = jnp.concatenate([keep_a + got_a.astype(jnp.float32), keep_b + got_b.astype(jnp.float32)], axis=1)
    h = residual[0].astype(jnp.float32) + attn
    row = t * rows + jnp.arange(rows, dtype=jnp.int32)
    live = (row < valid_tokens[0])[:, None]
    kept = jnp.where(live, h, 0.0)
    onward = [(s, s + 1) for s in range(sections - 1)]
    sending = kept.astype(jnp.bfloat16)
    square = jnp.sum(h * h, axis=1)[None]
    GATE = 0
    if GATE:
        begun = lax.ppermute(sending[:GATE], "section", onward)
        moved = jnp.concatenate([begun, lax.ppermute(sending[GATE:], "section", onward)])
        square = after(square, begun)
    else:
        moved = lax.ppermute(sending, "section", onward)
    square = lax.psum(square, "dp")
    scale = lax.rsqrt(square[0] / 8192.0 + 1e-06)
    gain = lax.dynamic_slice_in_dim(norm_gain[0], d * residual.shape[2], residual.shape[2])
    kept = after(kept, moved)
    normed = (kept * scale[:, None] * gain[None, :]).astype(jnp.bfloat16)
    return normed[None], moved[None]


def solution(mesh):
    placed = (
        P("section", "dp", "tensor"),
        P("section", "tensor", "dp"),
        P("section", "tensor", "dp"),
        P("section", None),
        P("section"),
    )
    return jax.shard_map(
        functools.partial(on_device, mesh.devices.shape[0]),
        mesh=mesh,
        in_specs=placed,
        out_specs=(P("section", "tensor", "dp"), P("section", "tensor", "dp")),
        check_vma=False,
    )
```
